32 devices in a mesh: dp: 2 (over x), expert: 16 (over z, y, core).
Axes of the slice: x: 2, y: 2, z: 4, core: 2. Of those that a mesh axis runs over, the one named last changes fastest.
Arguments:
- tokens: bfloat16 [2, 512, 4096], P(None, ('dp', 'expert')), may hold values from -6 to 6
- expert_ids: int32 [2, 512, 8], P(None, ('dp', 'expert')), may hold values from 0 to 15, all different within a row; in each aligned block of 16 rows (0 to 15, 16 to 31, ..., all dimensions but the last counted through in order) at most 9 rows name the same one
- gate_probs: float32 [2, 512, 8], P(None, ('dp', 'expert')), may hold values from 0.1 to 1
- gate_up: bfloat16 [16, 2, 768, 4096], P('expert', None, 'dp'), may hold values from -0.09375 to 0.09375
- down_proj: bfloat16 [16, 768, 4096], P('expert', 'dp'), may hold values from -0.21875 to 0.21875
- pairs: int32 [2, 2], replicated, may hold values from 0 to 15, as said below
Outputs:
- moe_out: bfloat16 [2, 512, 4096], P(None, ('dp', 'expert'))
- placed_gate_up: bfloat16 [16, 2, 768, 4096], P('expert', None, 'dp')
- placed_down: bfloat16 [16, 768, 4096], P('expert', 'dp')
The draws below stay inside these ranges and needn't reach their ends.
Inputs may be any that keep to these rules, and one draw needn't show every extreme that they name: `expert_ids`: in each step, the 16 rows of one device name one expert at most 9 times. `pairs`: each row is (j, j + 8) with j below 8; no slot stands in two rows.
All inputs are finite; a program needn't handle non-finite values.
Results may differ from the reference program's by a relative error of at most 0.012.
Values may be sent and summed in bfloat16 or wider, within the bound.
A program may use at most 128 MiB of HBM per device.

```python
import math
import jax
import jax.numpy as jnp
import numpy as np
from jax import lax

D = 4096
FF = 768
TOP = 8
STEPS = 2
ROWS_DEV = 16
EXPERTS = 16
TOKENS = 512
CAP = 9
HALF = 8
PAIRS = 2
N_DP = 2


def draw_pairs(key, part):
    middle = jax.random.permutation(key, jnp.arange(1, HALF - 1, dtype=jnp.int32))
    lower_dev = jnp.concatenate([jnp.array([0, HALF - 1], jnp.int32), middle[:PAIRS - 2]])
    order_key = jax.random.fold_in(key, 7)
    lower_dev = lower_dev[jax.random.permutation(order_key, PAIRS)]
    return jnp.stack([lower_dev, lower_dev + HALF], axis=1).astype(jnp.int32)


def steps_of(stream_key, extent, split, low, high):
    level = 1.0
    for position, shards_of in split:
        steps = jax.random.uniform(jax.random.fold_in(jax.random.fold_in(stream_key, 6), position), (shards_of,), jnp.float32, low / len(split), high / len(split))
        level = level * jnp.repeat(jnp.exp(steps), extent[position] // shards_of).reshape((-1,) + (1,) * (len(extent) - 1 - position))
    return level


def routed_block(rng, own, number, rows, number_of, top, reach, lean):
    ranking = jax.random.permutation(rng, number_of)
    crowded, usual = shares(number_of, rows * top, reach, lean, True), shares(number_of, rows * top, reach, lean, False)
    places = jnp.arange(number_of)

    def named(tallies, offset_by):
        used = int((tallies > 0).sum())
        fixed = max(1, used // 4)
        shifted = fixed + (places - fixed + offset_by * (used - fixed)) % max(1, number_of - fixed)
        return jnp.zeros((number_of,), jnp.int32).at[ranking[jnp.where(places < fixed, places, shifted)]].set(jnp.asarray(tallies, jnp.int32))

    tallies = jnp.where(number % 4 == 0, named(crowded, number // 4), named(usual, number - number // 4 - 1))
    mixed = jax.random.permutation(jax.random.fold_in(own, 3), number_of)
    giver, taker = mixed[0:number_of // 2 * 2:2], mixed[1:number_of // 2 * 2:2]
    margin = jnp.minimum(tallies[giver] - 1, reach - tallies[taker]) // 2
    margin = jnp.where((giver == ranking[0]) | (taker == ranking[0]) | (tallies[taker] == 0), 0, jnp.maximum(margin, 0))
    shifted = jax.random.randint(jax.random.fold_in(own, 4), (number_of // 2,), 0, 1 << 20) % (margin + 1)
    tallies = tallies.at[giver].add(-shifted).at[taker].add(shifted)
    items = jnp.searchsorted(jnp.cumsum(tallies), jnp.arange(rows * top), side="right").astype(jnp.int32)
    table = items.reshape(top, rows).T
    table = table[jax.random.permutation(jax.random.fold_in(own, 1), rows)]
    offset_by = jax.random.randint(jax.random.fold_in(own, 2), (rows, 1), 0, top)
    return jnp.take_along_axis(table, (jnp.arange(top)[None, :] + offset_by) % top, axis=1)


def shares(number_of, total, reach, lean, full):
    portions = [(1 << 20) // math.isqrt(rank ** lean) + 1 for rank in range(1, number_of + 1)]
    largest = reach if full else min(reach, max(-(-total // number_of), total * portions[0] // sum(portions)))
    least = 1 if total - largest >= number_of - 1 else 0
    counts, surplus = [largest] + [least] * (number_of - 1), total - largest - least * (number_of - 1)
    while surplus > 0:
        free = [i for i in range(1, number_of) if counts[i] < largest] or [i for i in range(1, number_of) if counts[i] < reach]
        pool, remaining = sum([portions[i] for i in free]), surplus
        for i in free:
            more = min(reach - counts[i], max(1, remaining * portions[i] // pool), surplus)
            counts[i] = counts[i] + more
            surplus = surplus - more
    return np.array(counts)


def scatter_about(stream_key, shape, scale, reach, split=(), kind=jnp.bfloat16):
    values = jax.random.normal(stream_key, shape, jnp.float32) * scale
    if len(split) > 0:
        values = steps_of(stream_key, shape, split, -0.22, 0.18) * values
    return jnp.clip(values, min=-reach, max=reach).astype(kind)


def setup_inputs(seed: int = 0) -> dict:
    key_list = jax.random.split(jax.random.key(seed), 7)
    tokens = scatter_about(key_list[0], (STEPS, TOKENS, D), 1.0, 6.0, ((1, 32),))
    expert_ids_keys = jax.random.split(jax.random.fold_in(key_list[1], 1), STEPS * TOKENS // ROWS_DEV)
    expert_ids_turns = jax.random.permutation(jax.random.fold_in(key_list[1], 3), STEPS * TOKENS // ROWS_DEV)
    expert_ids = jax.vmap(lambda own, number: routed_block(jax.random.fold_in(key_list[1], 2), own, number, ROWS_DEV, EXPERTS, TOP, CAP, 2))(expert_ids_keys, expert_ids_turns).reshape((STEPS, TOKENS, TOP))
    gate_probs = jnp.clip(0.1 + 0.9 * jax.random.uniform(key_list[2], (STEPS, TOKENS, TOP), jnp.float32) ** steps_of(key_list[2], (STEPS, TOKENS, TOP), ((1, 32),), -0.2, 0.2), 0.1, 1.0)
    gate_up = scatter_about(key_list[3], (EXPERTS, 2, FF, D), D ** -0.5, 0.09375, ((0, 16), (2, 2)))
    down_proj = scatter_about(key_list[4], (EXPERTS, FF, D), FF ** -0.5, 0.21875, ((0, 16), (1, 2)))
    pairs = draw_pairs(jax.random.fold_in(key_list[6], 71), 0)
    return {"tokens": tokens, "expert_ids": expert_ids, "gate_probs": gate_probs, "gate_up": gate_up, "down_proj": down_proj, "pairs": pairs}


def expert_rows(row_block, expert_gu, expert_down):
    dims = (((1,), (1,)), ((), ()))
    gate = lax.dot_general(row_block, expert_gu[0], dims, preferred_element_type=jnp.float32)
    upper = lax.dot_general(row_block, expert_gu[1], dims, preferred_element_type=jnp.float32)
    hidden = (jax.nn.silu(gate) * upper).astype(jnp.bfloat16)
    quarter = FF // N_DP
    total = jnp.zeros((row_block.shape[0], D), jnp.float32)
    for q_index in range(N_DP):
        piece = jnp.dot(hidden[:, q_index * quarter:(q_index + 1) * quarter],
                        expert_down[q_index * quarter:(q_index + 1) * quarter],
                        preferred_element_type=jnp.float32).astype(jnp.bfloat16)
        total = total + piece.astype(jnp.float32)
    return total.astype(jnp.bfloat16)


def one_step(step_tokens, step_ids, step_gates, gate_up, down_proj):
    flat_ids = step_ids.reshape(-1)
    flat_gates = step_gates.reshape(-1)
    slot_total = (TOKENS // ROWS_DEV) * CAP

    def per_expert(accum, expert_index):
        hit_mask = flat_ids == expert_index
        entry_idx = jnp.nonzero(hit_mask, size=slot_total, fill_value=0)[0].astype(jnp.int32)
        hit_count = jnp.sum(hit_mask.astype(jnp.int32))
        valid = jnp.arange(slot_total, dtype=jnp.int32) < hit_count
        token_idx = entry_idx // TOP
        row_block = jnp.take(step_tokens, token_idx, axis=0)
        expert_out = expert_rows(row_block, gate_up[expert_index], down_proj[expert_index])
        weights = jnp.where(valid, jnp.take(flat_gates, entry_idx), jnp.zeros((), flat_gates.dtype))
        accum = accum.at[token_idx].add(weights[:, None] * expert_out.astype(jnp.float32))
        return accum, None

    accum, _ = lax.scan(per_expert, jnp.zeros((TOKENS, D), jnp.float32), jnp.arange(EXPERTS, dtype=jnp.int32))
    return accum.astype(jnp.bfloat16)


def reference(tokens, expert_ids, gate_probs, gate_up, down_proj, pairs):
    results = jnp.stack([one_step(tokens[step_idx], expert_ids[step_idx], gate_probs[step_idx], gate_up, down_proj)
                         for step_idx in range(STEPS)])
    positions = jnp.arange(EXPERTS, dtype=jnp.int32)
    lower_dev = pairs[:, 0].astype(jnp.int32)
    upper_dev = pairs[:, 1].astype(jnp.int32)
    sigma = positions + jnp.sum(jnp.where(positions[:, None] == lower_dev[None, :], (upper_dev - lower_dev)[None, :], 0), axis=1)
    sigma = sigma + jnp.sum(jnp.where(positions[:, None] == upper_dev[None, :], (lower_dev - upper_dev)[None, :], 0), axis=1)
    sigma = sigma.astype(jnp.int32)
    return results, jnp.take(gate_up, sigma, axis=0), jnp.take(down_proj, sigma, axis=0)
```

```python
import jax
import jax.numpy as jnp
from jax import lax
from jax.sharding import PartitionSpec as P

LANES = 128
CHUNK_BYTES = 16 << 20


def expert_weights(expert_ids, gate_probs, expert_count):
    hot = expert_ids[..., None] == lax.iota(jnp.int32, expert_count)
    return jnp.sum(jnp.where(hot, gate_probs[..., None], 0.0), axis=-2)


def relocate(pair_low, gate_up, down_proj):
    slot_count = lax.axis_size("expert")
    half = slot_count // 2

    def branch(low):
        perm = [(low, low + half), (low + half, low)]
        return lambda operands: tuple(lax.ppermute(o, "expert", perm) for o in operands)

    return lax.switch(pair_low, [branch(j) for j in range(half)], (gate_up, down_proj))


def expert_share(gathered, gate_up, down_proj, me, expert_count):
    units, width = down_proj.shape
    side_width = gathered.shape[1] - width
    column = lax.iota(jnp.int32, side_width)
    pick = (column == me) | (column == me + expert_count)
    weight = jnp.sum(jnp.where(pick, gathered[:, width:].astype(jnp.float32), 0.0), axis=-1)
    projected = lax.dot_general(
        gathered[:, :width],
        gate_up.reshape(2 * units, width),
        (((1,), (1,)), ((), ())),
        preferred_element_type=jnp.float32,
    )
    hidden = (jax.nn.silu(projected[:, :units]) * projected[:, units:]).astype(jnp.bfloat16)
    partial = jnp.dot(hidden, down_proj, preferred_element_type=jnp.float32)
    return (partial * weight[:, None]).astype(jnp.bfloat16)


def local(tokens, expert_ids, gate_probs, gate_up, down_proj, pairs):
    steps, rows, width = tokens.shape
    expert_count = lax.axis_size("expert")
    me = lax.axis_index("expert")
    pair_count = pairs.shape[0]
    axes = ("dp", "expert")

    weights = expert_weights(expert_ids, gate_probs, expert_count)
    high = weights.astype(jnp.bfloat16)
    low = (weights - high.astype(jnp.float32)).astype(jnp.bfloat16)
    side_width = -(-2 * expert_count // LANES) * LANES
    side = jnp.concatenate([high, low], axis=-1)
    side = jnp.pad(side, ((0, 0), (0, 0), (0, side_width - 2 * expert_count)))
    packed = jnp.concatenate([tokens, side], axis=-1).reshape(steps * rows, width + side_width)
    row_bytes = 2 * width * steps * rows * lax.axis_size("dp") * expert_count
    parts = 1
    while row_bytes > parts * CHUNK_BYTES and steps * rows % (32 * parts) == 0:
        parts *= 2
    pieces = packed.reshape(parts, steps * rows // parts, width + side_width)
    gathered = lax.all_gather(pieces[0], axes, axis=0, tiled=True)
    got = [relocate(pairs[0, 0], gate_up, down_proj)]
    gathered, got = lax.optimization_barrier((gathered, got))

    outs = []
    for part in range(parts):
        if part:
            piece, outs[-1] = lax.optimization_barrier((pieces[part], outs[-1]))
            gathered = lax.all_gather(piece, axes, axis=0, tiled=True)
        partial = expert_share(gathered, gate_up[0], down_proj[0], me, expert_count)
        outs.append(lax.psum_scatter(partial, axes, scatter_dimension=0, tiled=True))
    got += [relocate(pairs[p, 0], gate_up, down_proj) for p in range(1, min(2, pair_count))]
    out = jnp.stack(outs).reshape(steps, rows, width)

    def place(pair, arrived, placed):
        mine = jnp.any(pair == me)
        return tuple(jnp.where(mine, new, old) for new, old in zip(arrived, placed))

    placed = (gate_up, down_proj)
    for p, arrived in enumerate(got):
        placed = place(pairs[p], arrived, placed)
    if pair_count > len(got):
        placed = lax.fori_loop(
            len(got),
            pair_count,
            lambda p, held: place(pairs[p], relocate(pairs[p, 0], gate_up, down_proj), held),
            placed,
        )
    placed_gu, placed_down = placed
    return out, placed_gu, placed_down


def solution(mesh):
    return jax.shard_map(
        local,
        mesh=mesh,
        in_specs=(
            P(None, ("dp", "expert"), None),
            P(None, ("dp", "expert"), None),
            P(None, ("dp", "expert"), None),
            P("expert", None, "dp", None),
            P("expert", "dp", None),
            P(),
        ),
        out_specs=(
            P(None, ("dp", "expert"), None),
            P("expert", None, "dp", None),
            P("expert", "dp", None),
        ),
        check_vma=False,
    )
```

```python
import jax
import jax.numpy as jnp
from jax import lax
from jax.sharding import PartitionSpec as P

LANES = 128
CHUNK_BYTES = 16 << 20


def expert_weights(expert_ids, gate_probs, expert_count):
    hot = expert_ids[..., None] == lax.iota(jnp.int32, expert_count)
    return jnp.sum(jnp.where(hot, gate_probs[..., None], 0.0), axis=-2)


def relocate(pair_low, weights):
    half = lax.axis_size("expert") // 2

    def branch(low):
        perm = [(low, low + half), (low + half, low)]
        return lambda operand: lax.ppermute(operand, "expert", perm)

    return lax.switch(pair_low, [branch(j) for j in range(half)], weights)


def expert_share(gathered, gate_up, down_proj, me, expert_count):
    units, width = down_proj.shape
    side_width = gathered.shape[1] - width
    column = lax.iota(jnp.int32, side_width)
    pick = (column == me) | (column == me + expert_count)
    weight = jnp.sum(jnp.where(pick, gathered[:, width:].astype(jnp.float32), 0.0), axis=-1)
    projected = lax.dot_general(
        gathered[:, :width],
        gate_up.reshape(2 * units, width),
        (((1,), (1,)), ((), ())),
        preferred_element_type=jnp.float32,
    )
    hidden = (jax.nn.silu(projected[:, :units]) * projected[:, units:]).astype(jnp.bfloat16)
    partial = jnp.dot(hidden, down_proj, preferred_element_type=jnp.float32)
    return (partial * weight[:, None]).astype(jnp.bfloat16)


def local(tokens, expert_ids, gate_probs, gate_up, down_proj, pairs):
    steps, rows, width = tokens.shape
    expert_count = lax.axis_size("expert")
    me = lax.axis_index("expert")
    pair_count = pairs.shape[0]
    axes = ("dp", "expert")

    weights = expert_weights(expert_ids, gate_probs, expert_count)
    high = weights.astype(jnp.bfloat16)
    low = (weights - high.astype(jnp.float32)).astype(jnp.bfloat16)
    side_width = -(-2 * expert_count // LANES) * LANES
    side = jnp.concatenate([high, low], axis=-1)
    side = jnp.pad(side, ((0, 0), (0, 0), (0, side_width - 2 * expert_count)))
    packed = jnp.concatenate([tokens, side], axis=-1).reshape(steps * rows, width + side_width)
    row_bytes = 2 * width * steps * rows * lax.axis_size("dp") * expert_count
    parts = 1
    while row_bytes > parts * CHUNK_BYTES and steps * rows % (32 * parts) == 0:
        parts *= 2
    pieces = packed.reshape(parts, steps * rows // parts, width + side_width)
    gathered = lax.all_gather(pieces[0], axes, axis=0, tiled=True)
    early_count = min(2, pair_count)
    got_down = [relocate(pairs[p, 0], down_proj) for p in range(early_count)]
    gathered, got_down = lax.optimization_barrier((gathered, got_down))

    outs = []
    for part in range(parts):
        if part:
            piece, outs[-1] = lax.optimization_barrier((pieces[part], outs[-1]))
            gathered = lax.all_gather(piece, axes, axis=0, tiled=True)
        partial = expert_share(gathered, gate_up[0], down_proj[0], me, expert_count)
        if part == parts - 1:
            partial, late_gu = lax.optimization_barrier((partial, gate_up))
        outs.append(lax.psum_scatter(partial, axes, scatter_dimension=0, tiled=True))
    got_gu = [relocate(pairs[p, 0], late_gu) for p in range(early_count)]
    out = jnp.stack(outs).reshape(steps, rows, width)

    def place(pair, arrived, held):
        return jnp.where(jnp.any(pair == me), arrived, held)

    placed_gu, placed_down = gate_up, down_proj
    for p in range(early_count):
        placed_gu = place(pairs[p], got_gu[p], placed_gu)
        placed_down = place(pairs[p], got_down[p], placed_down)
    if pair_count > early_count:
        placed_gu, placed_down = lax.fori_loop(
            early_count,
            pair_count,
            lambda p, held: (
                place(pairs[p], relocate(pairs[p, 0], gate_up), held[0]),
                place(pairs[p], relocate(pairs[p, 0], down_proj), held[1]),
            ),
            (placed_gu, placed_down),
        )
    return out, placed_gu, placed_down


def solution(mesh):
    return jax.shard_map(
        local,
        mesh=mesh,
        in_specs=(
            P(None, ("dp", "expert"), None),
            P(None, ("dp", "expert"), None),
            P(None, ("dp", "expert"), None),
            P("expert", None, "dp", None),
            P("expert", "dp", None),
            P(),
        ),
        out_specs=(
            P(None, ("dp", "expert"), None),
            P("expert", None, "dp", None),
            P("expert", "dp", None),
        ),
        check_vma=False,
    )
```
